32 devices in a mesh: pipe: 4 (over y, x), expert: 8 (over z, core).
Axes of the slice: x: 2, y: 2, z: 4, core: 2. Of those that a mesh axis runs over, the one named last changes fastest.
Arguments:
- fwd_acts: bfloat16 [4, 1024, 3584], P('pipe', 'expert'), may hold values from -6 to 6
- bwd_saved: bfloat16 [4, 1024, 3584], P('pipe', 'expert'), may hold values from -6 to 6
- bwd_grads: bfloat16 [4, 1024, 3584], P('pipe', 'expert'), may hold values from -6 to 6
- norm_gain: float32 [4, 3584], P('pipe'), may hold values from 0.1 to 1.9
- router: bfloat16 [4, 3584, 4], P('pipe'), may hold values from -0.09375 to 0.09375
- w_up: bfloat16 [4, 3584, 4096], P('pipe', None, 'expert'), may hold values from -0.09375 to 0.09375
- w_down: bfloat16 [4, 4096, 3584], P('pipe', 'expert'), may hold values from -0.1875 to 0.1875
- fwd_experts: int32 [4, 1024, 2], P('pipe', 'expert'), may hold values from 0 to 3, all different within a row; in each aligned block of 128 rows (0 to 127, 128 to 255, ..., all dimensions but the last counted through in order) at most 72 rows name the same one
- bwd_experts: int32 [4, 1024, 2], P('pipe', 'expert'), may hold values from 0 to 3, all different within a row; in each aligned block of 128 rows (0 to 127, 128 to 255, ..., all dimensions but the last counted through in order) at most 72 rows name the same one
Outputs:
- fwd_next: bfloat16 [4, 1024, 3584], P('pipe', 'expert')
- bwd_next: bfloat16 [4, 1024, 3584], P('pipe', 'expert')
The draws below stay inside these ranges and needn't reach their ends.
Inputs may be any that keep to these rules, and one draw needn't show every extreme that they name: `fwd_experts`: each row names 2 different experts. Within the 128 rows of one device no expert is named by more than 72 rows, and in every draw some expert is named by exactly 72 rows of some device. `bwd_experts`: each row names 2 different experts. Within the 128 rows of one device no expert is named by more than 72 rows, and in every draw some expert is named by exactly 72 rows of some device.
All inputs are finite; a program needn't handle non-finite values.
Results may differ from the reference program's by a relative error of at most 0.0069.
Values may be sent and summed in bfloat16 or wider, within the bound.
A program may use at most 192 MiB of HBM per device.

```python
import math
import jax
import jax.numpy as jnp
import numpy as np
from jax import lax

D = 3584
FF = 1024
HALVES = 2
TOP = 2
TOK_DEV = 128
EXPERTS = 4
CAP = 72
SECTIONS = 4
TOKENS = 1024
N_EXPERT = 8


def level_of(rng, shape, split, smallest, largest):
    def one(axis_at, shards_of):
        heights = jax.random.uniform(jax.random.fold_in(jax.random.fold_in(rng, 6), axis_at), (shards_of,), jnp.float32, smallest / len(split), largest / len(split))
        return jnp.repeat(jnp.exp(heights), shape[axis_at] // shards_of).reshape((-1,) + (1,) * (len(shape) - axis_at - 1))

    level = one(*split[0])
    for cut in split[1:]:
        level = level * one(*cut)
    return level


def deal_out(rng, own, number, rows, amount, top, most, lean):
    sequence = jax.random.permutation(rng, amount)
    crowded, ordinary = shares(amount, rows * top, most, lean, True), shares(amount, rows * top, most, lean, False)
    places = jnp.arange(amount)

    def named(sizes, offset_by):
        used = int((sizes > 0).sum())
        fixed = max(1, used // 4)
        shifted = fixed + (places - fixed + offset_by * (used - fixed)) % max(1, amount - fixed)
        return jnp.zeros((amount,), jnp.int32).at[sequence[jnp.where(places < fixed, places, shifted)]].set(jnp.asarray(sizes, jnp.int32))

    sizes = jnp.where(number % 4 == 0, named(crowded, number // 4), named(ordinary, number - number // 4 - 1))
    mixed = jax.random.permutation(jax.random.fold_in(own, 3), amount)
    giver, taker = mixed[0:amount // 2 * 2:2], mixed[1:amount // 2 * 2:2]
    slack = jnp.minimum(sizes[giver] - 1, most - sizes[taker]) // 2
    slack = jnp.where((giver == sequence[0]) | (taker == sequence[0]) | (sizes[taker] == 0), 0, jnp.maximum(slack, 0))
    shifted = jax.random.randint(jax.random.fold_in(own, 4), (amount // 2,), 0, 1 << 20) % (slack + 1)
    sizes = sizes.at[giver].add(-shifted).at[taker].add(shifted)
    items = jnp.searchsorted(jnp.cumsum(sizes), jnp.arange(rows * top), side="right").astype(jnp.int32)
    grid = items.reshape(top, rows).T
    grid = grid[jax.random.permutation(jax.random.fold_in(own, 1), rows)]
    offset_by = jax.random.randint(jax.random.fold_in(own, 2), (rows, 1), 0, top)
    return jnp.take_along_axis(grid, (jnp.arange(top)[None, :] + offset_by) % top, axis=1)


def shares(count, total, bound, slope, full):
    weights = [(1 << 20) // math.isqrt(standing ** slope) + 1 for standing in range(1, count + 1)]
    largest = bound if full else min(bound, max(-(-total // count), total * weights[0] // sum(weights)))
    least = 1 if total - largest >= count - 1 else 0
    given, rest = [largest] + [least] * (count - 1), total - largest - least * (count - 1)
    while rest > 0:
        movable = [i for i in range(1, count) if given[i] < largest] or [i for i in range(1, count) if given[i] < bound]
        mass, left = sum([weights[i] for i in movable]), rest
        for i in movable:
            extra = min(bound - given[i], max(1, left * weights[i] // mass), rest)
            given[i] = given[i] + extra
            rest = rest - extra
    return np.array(given)


def bell_draw(stream_key, shape, spread, most, pieces=(), kind=jnp.bfloat16):
    drawn = jax.random.normal(stream_key, shape, jnp.float32) * spread
    if len(pieces) > 0:
        drawn = level_of(stream_key, shape, pieces, -0.22, 0.18) * drawn
    return jnp.clip(drawn, min=-most, max=most).astype(kind)


def setup_inputs(seed: int = 0) -> dict:
    key_list = jax.random.split(jax.random.key(seed), 10)
    fwd_acts = bell_draw(key_list[0], (SECTIONS, TOKENS, D), 1.0, 6.0, ((0, 4), (1, 8)))
    bwd_saved = bell_draw(key_list[1], (SECTIONS, TOKENS, D), 1.0, 6.0, ((0, 4), (1, 8)))
    bwd_grads = bell_draw(key_list[2], (SECTIONS, TOKENS, D), 1.0, 6.0, ((0, 4), (1, 8)))
    norm_gain = jnp.clip(1.0 + 0.18 * jax.random.normal(key_list[3], (SECTIONS, D), jnp.float32), 0.1, 1.9)
    router = bell_draw(key_list[4], (SECTIONS, D, EXPERTS), D ** -0.5, 0.09375, ((0, 4),))
    w_up = bell_draw(key_list[5], (SECTIONS, D, EXPERTS * FF), D ** -0.5, 0.09375, ((0, 4), (2, 8)))
    w_down = bell_draw(key_list[6], (SECTIONS, EXPERTS * FF, D), FF ** -0.5, 0.1875, ((0, 4), (1, 8)))
    fwd_experts_keys = jax.random.split(jax.random.fold_in(key_list[7], 1), SECTIONS * TOKENS // TOK_DEV)
    fwd_experts_turns = jax.random.permutation(jax.random.fold_in(key_list[7], 3), SECTIONS * TOKENS // TOK_DEV)
    fwd_experts = jax.vmap(lambda own, number: deal_out(jax.random.fold_in(key_list[7], 2), own, number, TOK_DEV, EXPERTS, TOP, CAP, 2))(fwd_experts_keys, fwd_experts_turns).reshape((SECTIONS, TOKENS, TOP))
    bwd_experts_keys = jax.random.split(jax.random.fold_in(key_list[8], 1), SECTIONS * TOKENS // TOK_DEV)
    bwd_experts_turns = jax.random.permutation(jax.random.fold_in(key_list[8], 3), SECTIONS * TOKENS // TOK_DEV)
    bwd_experts = jax.vmap(lambda own, number: deal_out(jax.random.fold_in(key_list[8], 2), own, number, TOK_DEV, EXPERTS, TOP, CAP, 2))(bwd_experts_keys, bwd_experts_turns).reshape((SECTIONS, TOKENS, TOP))
    return dict(fwd_acts=fwd_acts, bwd_saved=bwd_saved, bwd_grads=bwd_grads, norm_gain=norm_gain, router=router, w_up=w_up, w_down=w_down, fwd_experts=fwd_experts, bwd_experts=bwd_experts)


EPS = 1e-06
ROUTE_SCALE = 2.5

def normalize(acts, gain):
    wide = acts.astype(jnp.float32)
    inverse = lax.rsqrt(lax.optimization_barrier(jnp.mean(wide * wide, axis=-1, keepdims=True)) + EPS)
    return (wide, inverse, (wide * inverse * gain).astype(jnp.bfloat16))

def gating(normed, table, choose):
    logits = jnp.dot(normed, table, preferred_element_type=jnp.float32)
    affinity = jax.nn.sigmoid(logits)
    onehot = (choose[:, :, None] == jnp.arange(table.shape[1], dtype=jnp.int32)[None, None, :]).astype(jnp.float32)
    picked = lax.optimization_barrier(jnp.sum(onehot * affinity[:, None, :], axis=2))
    total = lax.optimization_barrier(jnp.sum(picked, axis=1, keepdims=True))
    return (onehot, picked, total, ROUTE_SCALE * picked / total)

def slot_of(choose, experts):
    flat = choose.reshape(-1)
    onehot = (flat[:, None] == jnp.arange(experts, dtype=jnp.int32)[None, :]).astype(jnp.int32)
    before = jnp.cumsum(onehot, axis=0) - onehot
    return lax.optimization_barrier(jnp.sum(before * onehot, axis=1)).astype(jnp.int32)

def dispatch_rows(rows, owner, where, count):
    fill = jnp.full((count,), rows.shape[0], jnp.int32).at[where].set(owner.astype(jnp.int32))
    padded = jnp.concatenate([rows, jnp.zeros((1, rows.shape[1]), rows.dtype)], axis=0)
    return jnp.take(padded, fill, axis=0)

def expert_forward(rows, up, down):
    pre = jnp.dot(rows, up, preferred_element_type=jnp.float32)
    hidden = jax.nn.silu(pre).astype(jnp.bfloat16)
    return jnp.dot(hidden, down, preferred_element_type=jnp.float32).astype(jnp.bfloat16)

def expert_backward(rows, grads, up, down):
    pre = jnp.dot(rows, up, preferred_element_type=jnp.float32)
    sigma = jax.nn.sigmoid(pre)
    hidden = (pre * sigma).astype(jnp.bfloat16)
    output = jnp.dot(hidden, down, preferred_element_type=jnp.float32).astype(jnp.bfloat16)
    back = lax.dot_general(grads, down, (((1,), (1,)), ((), ())), preferred_element_type=jnp.float32)
    dpre = (back * sigma * (1.0 + pre * (1.0 - sigma))).astype(jnp.bfloat16)
    dinput = lax.dot_general(dpre, up, (((1,), (1,)), ((), ())), preferred_element_type=jnp.float32)
    return (output, dinput.astype(jnp.bfloat16))

def router_grad(grads, routed, onehot, picked, total, table):
    dgate = lax.optimization_barrier(jnp.sum(routed.astype(jnp.float32) * grads.astype(jnp.float32)[:, None, :], axis=2))
    dsel = ROUTE_SCALE / total * (dgate - lax.optimization_barrier(jnp.sum(dgate * picked, axis=1, keepdims=True)) / total)
    dlogit = lax.optimization_barrier(jnp.sum(onehot * (dsel * picked * (1.0 - picked))[:, :, None], axis=1))
    return jnp.dot(dlogit, table.astype(jnp.float32).T, precision=lax.Precision.HIGHEST)

def norm_grad(grads, dnormed, wide, inverse, gain):
    scaled = dnormed * gain
    inner = lax.optimization_barrier(jnp.mean(scaled * wide, axis=-1, keepdims=True))
    return (grads.astype(jnp.float32) + inverse * scaled - wide * inverse ** 3 * inner).astype(jnp.bfloat16)

def split_weights(up, down):
    ups = up.reshape(D, EXPERTS, HALVES, FF // HALVES).transpose(1, 2, 0, 3)
    downs = down.reshape(EXPERTS, HALVES, FF // HALVES, D)
    return (ups, downs)

def experts_forward(buffer, ups, downs):

    def one_expert(item):
        rows, up_e, down_e = item
        total = jnp.zeros(rows.shape, jnp.float32)
        for half in range(HALVES):
            total = total + expert_forward(rows, up_e[half], down_e[half]).astype(jnp.float32)
        return total.astype(jnp.bfloat16)
    return lax.map(one_expert, (buffer, ups, downs))

def experts_backward(buffer, grad_buffer, ups, downs):

    def one_expert(item):
        rows, grads, up_e, down_e = item
        out_total = jnp.zeros(rows.shape, jnp.float32)
        in_total = jnp.zeros(rows.shape, jnp.float32)
        for half in range(HALVES):
            output, dinput = expert_backward(rows, grads, up_e[half], down_e[half])
            out_total = out_total + output.astype(jnp.float32)
            in_total = in_total + dinput.astype(jnp.float32)
        return (out_total.astype(jnp.bfloat16), in_total.astype(jnp.bfloat16))
    return lax.map(one_expert, (buffer, grad_buffer, ups, downs))

def placement_of(choose, block):
    slots = jax.vmap(lambda c: slot_of(c, EXPERTS))(choose.reshape(N_EXPERT, TOK_DEV, TOP)).reshape(-1)
    return ((choose.reshape(-1) * N_EXPERT + block) * CAP + slots).astype(jnp.int32)

def reference(fwd_acts, bwd_saved, bwd_grads, norm_gain, router, w_up, w_down, fwd_experts, bwd_experts):
    count = TOKENS * TOP
    block = jnp.arange(count, dtype=jnp.int32) // (TOK_DEV * TOP)
    owner = jnp.arange(count, dtype=jnp.int32) // TOP
    every = jnp.arange(count, dtype=jnp.int32)
    room = EXPERTS * N_EXPERT * CAP
    forward_outs = []
    backward_outs = []
    for section in range(SECTIONS):
        gain = norm_gain[section]
        table = router[section]
        ups, downs = split_weights(w_up[section], w_down[section])
        choose = fwd_experts[section]
        wide, inverse, normed = normalize(fwd_acts[section], gain)
        onehot, picked, total, gate = gating(normed, table, choose)
        where = placement_of(choose, block)
        buffer = dispatch_rows(normed, owner, where, room).reshape(EXPERTS, N_EXPERT * CAP, D)
        result = experts_forward(buffer, ups, downs)
        routed = jnp.take(result.reshape(-1, D), where, axis=0).reshape(TOKENS, TOP, D)
        moe = lax.optimization_barrier(jnp.sum(gate[:, :, None] * routed.astype(jnp.float32), axis=1))
        forward_outs.append((wide + moe).astype(jnp.bfloat16))
        choose = bwd_experts[section]
        grads = bwd_grads[section]
        wide, inverse, normed = normalize(bwd_saved[section], gain)
        onehot, picked, total, gate = gating(normed, table, choose)
        where = placement_of(choose, block)
        scaled = (gate[:, :, None] * grads.astype(jnp.float32)[:, None, :]).astype(jnp.bfloat16).reshape(count, D)
        buffer = dispatch_rows(normed, owner, where, room).reshape(EXPERTS, N_EXPERT * CAP, D)
        grad_buffer = dispatch_rows(scaled, every, where, room).reshape(EXPERTS, N_EXPERT * CAP, D)
        result, dresult = experts_backward(buffer, grad_buffer, ups, downs)
        routed = jnp.take(result.reshape(-1, D), where, axis=0).reshape(TOKENS, TOP, D)
        droutes = jnp.take(dresult.reshape(-1, D), where, axis=0).reshape(TOKENS, TOP, D)
        dnormed = lax.optimization_barrier(jnp.sum(droutes.astype(jnp.float32), axis=1)) + router_grad(grads, routed, onehot, picked, total, table)
        backward_outs.append(norm_grad(grads, dnormed, wide, inverse, gain))
    return (jnp.roll(jnp.stack(forward_outs), 1, axis=0), jnp.roll(jnp.stack(backward_outs), -1, axis=0))
```

```python
import jax
import jax.numpy as jnp
from jax import lax
from jax.sharding import PartitionSpec as P

HALVES = 2
EPS = 1e-06
ROUTE_SCALE = 2.5


def partner(shard, axis, bit):
    return lax.ppermute(shard, axis, [(i, i ^ 1 << bit) for i in range(lax.axis_size(axis))])


def passed_along(block, axis, distance):
    devices = range(lax.axis_size(axis))
    route = [((i - distance) % len(devices), i) for i in devices]
    return lax.ppermute(block, axis, route)


def normalize(acts, gain):
    wide = acts.astype(jnp.float32)
    inverse = lax.rsqrt(jnp.mean(wide * wide, axis=-1, keepdims=True) + EPS)
    return (wide, inverse, (wide * inverse * gain).astype(jnp.bfloat16))


def gating(normed, table, choose):
    logits = jnp.dot(normed, table, preferred_element_type=jnp.float32)
    affinity = jax.nn.sigmoid(logits)
    onehot = (
        choose[:, :, None] == jnp.arange(table.shape[1], dtype=jnp.int32)[None, None, :]
    ).astype(jnp.float32)
    picked = jnp.sum(onehot * affinity[:, None, :], axis=2)
    total = jnp.sum(picked, axis=1, keepdims=True)
    return (onehot, picked, total, ROUTE_SCALE * picked / total)


def slot_masks(choose, experts, capacity):
    tok_rows, top = choose.shape
    flat = choose.reshape(-1)
    count = tok_rows * top
    onehot = (flat[:, None] == jnp.arange(experts, dtype=jnp.int32)[None, :]).astype(jnp.bfloat16)
    at = jnp.arange(count, dtype=jnp.int32)
    earlier = (at[None, :] < at[:, None]).astype(jnp.bfloat16)
    before = jnp.dot(earlier, onehot, preferred_element_type=jnp.float32)
    slot = jnp.sum(before * onehot.astype(jnp.float32), axis=1).astype(jnp.int32)
    where = (flat * capacity + slot).reshape(tok_rows, top)
    places = jnp.arange(experts * capacity, dtype=jnp.int32)
    return [(places[:, None] == where[None, :, k]).astype(jnp.bfloat16) for k in range(top)]


def pick(mask, rows):
    return jnp.dot(mask, rows, preferred_element_type=jnp.float32).astype(jnp.bfloat16)


def back_to_tokens(mask, rows):
    return lax.dot_general(
        mask, rows, (((0,), (0,)), ((), ())), preferred_element_type=jnp.float32
    )


def swap(rows):
    return lax.all_to_all(rows, "expert", split_axis=0, concat_axis=0, tiled=True)


def on_device(
    fwd_acts, bwd_saved, bwd_grads, norm_gain, router, w_up, w_down, fwd_experts, bwd_experts
):
    gain = norm_gain[0]
    table = router[0]
    width = fwd_acts.shape[2]
    tok_rows = fwd_acts.shape[1]
    experts = table.shape[1]
    top = fwd_experts.shape[2]
    capacity = 9 * tok_rows * top // (8 * experts)
    half_cap = capacity // HALVES
    devices = lax.axis_size("expert")
    shape = (devices, half_cap, width)
    ups = [w_up[0], partner(w_up[0], "expert", 0)]
    downs = [w_down[0], partner(w_down[0], "expert", 0)]

    choose_a = fwd_experts[0]
    masks_a = slot_masks(choose_a, experts, capacity)
    wide_a, inv_a, normed_a = normalize(fwd_acts[0], gain)
    got_a = swap(pick(sum(masks_a), normed_a).reshape(shape)).reshape(-1, width)
    _, _, _, gate_a = gating(normed_a, table, choose_a)

    choose_b = bwd_experts[0]
    grads_b = bwd_grads[0]
    masks_b = slot_masks(choose_b, experts, capacity)
    wide_b, inv_b, normed_b = normalize(bwd_saved[0], gain)
    spread = sum(masks_b)
    got_x = swap(pick(spread, normed_b).reshape(shape)).reshape(-1, width)
    got_g = swap(pick(spread, grads_b).reshape(shape)).reshape(-1, width)
    onehot_b, picked_b, total_b, gate_b = gating(normed_b, table, choose_b)

    y = jnp.zeros((devices * half_cap, width), jnp.float32)
    for up, down in zip(ups, downs):
        hidden = jax.nn.silu(jnp.dot(got_a, up, preferred_element_type=jnp.float32))
        y += jnp.dot(hidden.astype(jnp.bfloat16), down, preferred_element_type=jnp.float32)
    back_a = swap(y.astype(jnp.bfloat16).reshape(shape)).reshape(-1, width)

    dx = jnp.zeros((devices * half_cap, width), jnp.float32)
    dgate_rows = jnp.zeros((devices * half_cap,), jnp.float32)
    for up, down in zip(ups, downs):
        pre = jnp.dot(got_x, up, preferred_element_type=jnp.float32)
        sigma = jax.nn.sigmoid(pre)
        hidden = (pre * sigma).astype(jnp.bfloat16).astype(jnp.float32)
        back = lax.dot_general(
            got_g, down, (((1,), (1,)), ((), ())), preferred_element_type=jnp.float32
        )
        dgate_rows += jnp.sum(hidden * back, axis=1)
        dpre = (back * sigma * (1.0 + pre * (1.0 - sigma))).astype(jnp.bfloat16)
        dx += lax.dot_general(dpre, up, (((1,), (1,)), ((), ())), preferred_element_type=jnp.float32)
    back_g = swap(dgate_rows.reshape(devices, half_cap)).reshape(-1)
    back_x = swap(dx.astype(jnp.bfloat16).reshape(shape)).reshape(-1, width)

    out_a = wide_a
    for k in range(top):
        out_a = out_a + gate_a[:, k : k + 1] * back_to_tokens(masks_a[k], back_a)
    fwd_next = passed_along(out_a.astype(jnp.bfloat16)[None], "pipe", 1)

    dgate = jnp.stack(
        [jnp.sum(m.astype(jnp.float32) * back_g[:, None], axis=0) for m in masks_b], axis=1
    )
    dsel = ROUTE_SCALE / total_b * (
        dgate - jnp.sum(dgate * picked_b, axis=1, keepdims=True) / total_b
    )
    dlogit = jnp.sum(onehot_b * (dsel * picked_b * (1.0 - picked_b))[:, :, None], axis=1)
    dnormed = jnp.dot(dlogit, table.astype(jnp.float32).T, precision=lax.Precision.HIGHEST)
    for k in range(top):
        dnormed = dnormed + gate_b[:, k : k + 1] * back_to_tokens(masks_b[k], back_x)
    scaled = dnormed * gain
    inner = jnp.mean(scaled * wide_b, axis=-1, keepdims=True)
    dx_b = grads_b.astype(jnp.float32) + inv_b * scaled - wide_b * inv_b**3 * inner
    bwd_next = passed_along(dx_b.astype(jnp.bfloat16)[None], "pipe", -1)
    return (fwd_next, bwd_next)


def solution(mesh):
    placed = (
        P("pipe", "expert", None),
        P("pipe", "expert", None),
        P("pipe", "expert", None),
        P("pipe", None),
        P("pipe", None, None),
        P("pipe", None, "expert"),
        P("pipe", "expert", None),
        P("pipe", "expert", None),
        P("pipe", "expert", None),
    )
    return jax.shard_map(
        on_device,
        mesh=mesh,
        in_specs=placed,
        out_specs=(P("pipe", "expert", None), P("pipe", "expert", None)),
        check_vma=False,
    )
```

```python
import jax
import jax.numpy as jnp
from jax import lax
from jax.sharding import PartitionSpec as P

HALVES = 2
EPS = 1e-06
ROUTE_SCALE = 2.5


def partner(shard, axis, bit):
    return lax.ppermute(shard, axis, [(i, i ^ 1 << bit) for i in range(lax.axis_size(axis))])


def passed_along(block, axis, distance):
    devices = range(lax.axis_size(axis))
    route = [((i - distance) % len(devices), i) for i in devices]
    return lax.ppermute(block, axis, route)


def normalize(acts, gain):
    wide = acts.astype(jnp.float32)
    inverse = lax.rsqrt(jnp.mean(wide * wide, axis=-1, keepdims=True) + EPS)
    return (wide, inverse, (wide * inverse * gain).astype(jnp.bfloat16))


def gating(normed, table, choose):
    logits = jnp.dot(normed, table, preferred_element_type=jnp.float32)
    affinity = jax.nn.sigmoid(logits)
    onehot = (
        choose[:, :, None] == jnp.arange(table.shape[1], dtype=jnp.int32)[None, None, :]
    ).astype(jnp.float32)
    picked = jnp.sum(onehot * affinity[:, None, :], axis=2)
    total = jnp.sum(picked, axis=1, keepdims=True)
    return (onehot, picked, total, ROUTE_SCALE * picked / total)


ROWS = 16


class Layout:
    def __init__(self, width, half_cap, devices):
        self.width, self.half_cap, self.devices = width, half_cap, devices
        self.full, self.left = half_cap // ROWS, half_cap % ROWS
        self.pieces = ROWS // self.left if self.left else 1
        if self.left and (ROWS % self.left or width % (128 * self.pieces)):
            self.full, self.left, self.pieces = self.full + 1, 0, 1
        self.part = width // self.pieces
        self.columns = self.full * width + (self.part if self.left else 0)

    def masks(self, where):
        block = jnp.arange(self.devices * ROWS, dtype=jnp.int32)
        to, row = lax.axis_index("expert") ^ (block // ROWS), block % ROWS
        first = to * self.half_cap
        found = []
        for group in range(self.full):
            slot = group * ROWS + row
            place = jnp.where(slot < self.half_cap, first + slot, -1)
            found.append((place[:, None] == where[None, :]).astype(jnp.bfloat16))
        for piece in range(self.pieces if self.left else 0):
            slot = self.full * ROWS + row % self.left
            place = jnp.where(row // self.left == piece, first + slot, -1)
            found.append((place[:, None] == where[None, :]).astype(jnp.bfloat16))
        return found

    def parts(self, rows):
        return [rows[:, c * self.part : (c + 1) * self.part] for c in range(self.pieces)]

    def dispatch(self, masks, rows):
        cols = [pick(m, rows) for m in masks[: self.full]]
        if self.left:
            cols.append(
                pick(
                    jnp.concatenate(masks[self.full :], axis=1),
                    jnp.concatenate(self.parts(rows), axis=0),
                )
            )
        return jnp.concatenate(cols, axis=1)

    def lifts(self):
        slot = jnp.arange(self.devices * self.left, dtype=jnp.int32)
        block = jnp.arange(self.devices * ROWS, dtype=jnp.int32)
        at = (slot // self.left) * ROWS + slot % self.left
        return [
            (at[:, None] + c * self.left == block[None, :]).astype(jnp.bfloat16)
            for c in range(self.pieces)
        ]

    def unpack(self, packed):
        rows = [packed[:, g * self.width : (g + 1) * self.width] for g in range(self.full)]
        if self.left:
            tail = packed[:, self.full * self.width : self.columns]
            rows.append(jnp.concatenate([pick(m, tail) for m in self.lifts()], axis=1))
        return jnp.concatenate(rows, axis=0)

    def pack(self, rows):
        size = self.devices * ROWS
        cols = [rows[g * size : (g + 1) * size] for g in range(self.full)]
        if self.left:
            tail = rows[self.full * size :]
            cols.append(
                sum(back_to_tokens(m, p) for m, p in zip(self.lifts(), self.parts(tail))).astype(
                    jnp.bfloat16
                )
            )
        return jnp.concatenate(cols, axis=1)

    def numbers(self, values):
        size = self.devices * ROWS
        cols = [values[g * size : (g + 1) * size] for g in range(self.full)]
        if self.left:
            tail = values[self.full * size :]
            cols.append(jnp.sum(self.lifts()[0].astype(jnp.float32) * tail[:, None], axis=0))
        both = jnp.stack(cols, axis=1)
        high = lax.reduce_precision(both, 8, 7)
        split = jnp.concatenate([high, both - high], axis=1)
        return jnp.pad(split, ((0, 0), (0, -split.shape[1] % 128))).astype(jnp.bfloat16)

    def numbers_home(self, masks, split):
        count = self.full + (1 if self.left else 0)
        wide = split.astype(jnp.float32)
        return sum(
            jnp.sum(masks[g].astype(jnp.float32) * (wide[:, g] + wide[:, count + g])[:, None], axis=0)
            for g in range(count)
        )

    def home(self, masks, packed):
        out = sum(
            back_to_tokens(masks[g], packed[:, g * self.width : (g + 1) * self.width])
            for g in range(self.full)
        )
        if self.left:
            tail = packed[:, self.full * self.width : self.columns]
            out = out + jnp.concatenate(
                [back_to_tokens(m, tail) for m in masks[self.full :]], axis=1
            )
        return out

    def swap(self, packed):
        got = [packed[:ROWS]]
        for j in range(1, self.devices):
            route = [(i, i ^ j) for i in range(self.devices)]
            got.append(lax.ppermute(packed[j * ROWS : (j + 1) * ROWS], "expert", route))
        return jnp.concatenate(got, axis=0)


def slots_of(choose, experts, capacity):
    tok_rows, top = choose.shape
    flat = choose.reshape(-1)
    onehot = (flat[:, None] == jnp.arange(experts, dtype=jnp.int32)[None, :]).astype(jnp.bfloat16)
    at = jnp.arange(tok_rows * top, dtype=jnp.int32)
    earlier = (at[None, :] < at[:, None]).astype(jnp.bfloat16)
    before = jnp.dot(earlier, onehot, preferred_element_type=jnp.float32)
    slot = jnp.sum(before * onehot.astype(jnp.float32), axis=1).astype(jnp.int32)
    return (flat * capacity + slot).reshape(tok_rows, top)


def pick(mask, rows):
    return jnp.dot(mask, rows, preferred_element_type=jnp.float32).astype(jnp.bfloat16)


def back_to_tokens(mask, rows):
    return lax.dot_general(mask, rows, (((0,), (0,)), ((), ())), preferred_element_type=jnp.float32)


def on_device(
    fwd_acts, bwd_saved, bwd_grads, norm_gain, router, w_up, w_down, fwd_experts, bwd_experts
):
    gain = norm_gain[0]
    table = router[0]
    width = fwd_acts.shape[2]
    tok_rows = fwd_acts.shape[1]
    experts = table.shape[1]
    top = fwd_experts.shape[2]
    capacity = 9 * tok_rows * top // (8 * experts)
    half_cap = capacity // HALVES
    devices = lax.axis_size("expert")
    plan = Layout(width, half_cap, devices)
    ups = [w_up[0], partner(w_up[0], "expert", 0)]
    downs = [w_down[0], partner(w_down[0], "expert", 0)]

    choose_a = fwd_experts[0]
    where_a = slots_of(choose_a, experts, capacity)
    masks_a = [plan.masks(where_a[:, k]) for k in range(top)]
    wide_a, inv_a, normed_a = normalize(fwd_acts[0], gain)
    spread_a = [sum(each) for each in zip(*masks_a)]
    got_a = plan.unpack(plan.swap(plan.dispatch(spread_a, normed_a)))
    _, _, _, gate_a = gating(normed_a, table, choose_a)

    choose_b = bwd_experts[0]
    grads_b = bwd_grads[0]
    where_b = slots_of(choose_b, experts, capacity)
    masks_b = [plan.masks(where_b[:, k]) for k in range(top)]
    wide_b, inv_b, normed_b = normalize(bwd_saved[0], gain)
    spread_b = [sum(each) for each in zip(*masks_b)]
    got_x = plan.unpack(plan.swap(plan.dispatch(spread_b, normed_b)))
    got_g = plan.unpack(plan.swap(plan.dispatch(spread_b, grads_b)))
    onehot_b, picked_b, total_b, gate_b = gating(normed_b, table, choose_b)

    y = jnp.zeros((got_a.shape[0], width), jnp.float32)
    for up, down in zip(ups, downs):
        hidden = jax.nn.silu(jnp.dot(got_a, up, preferred_element_type=jnp.float32))
        y += jnp.dot(hidden.astype(jnp.bfloat16), down, preferred_element_type=jnp.float32)
    back_a = plan.swap(plan.pack(y.astype(jnp.bfloat16)))

    dx = jnp.zeros((got_a.shape[0], width), jnp.float32)
    dgate_rows = jnp.zeros((got_a.shape[0],), jnp.float32)
    for up, down in zip(ups, downs):
        pre = jnp.dot(got_x, up, preferred_element_type=jnp.float32)
        sigma = jax.nn.sigmoid(pre)
        hidden = (pre * sigma).astype(jnp.bfloat16).astype(jnp.float32)
        back = lax.dot_general(
            got_g, down, (((1,), (1,)), ((), ())), preferred_element_type=jnp.float32
        )
        dgate_rows += jnp.sum(hidden * back, axis=1)
        dpre = (back * sigma * (1.0 + pre * (1.0 - sigma))).astype(jnp.bfloat16)
        dx += lax.dot_general(dpre, up, (((1,), (1,)), ((), ())), preferred_element_type=jnp.float32)
    back_x = plan.swap(
        jnp.concatenate([plan.pack(dx.astype(jnp.bfloat16)), plan.numbers(dgate_rows)], axis=1)
    )

    out_a = wide_a
    for k in range(top):
        out_a = out_a + gate_a[:, k : k + 1] * plan.home(masks_a[k], back_a)
    fwd_next = passed_along(out_a.astype(jnp.bfloat16)[None], "pipe", 1)

    split = back_x[:, plan.columns :]
    dgate = jnp.stack([plan.numbers_home(m, split) for m in masks_b], axis=1)
    dsel = ROUTE_SCALE / total_b * (
        dgate - jnp.sum(dgate * picked_b, axis=1, keepdims=True) / total_b
    )
    dlogit = jnp.sum(onehot_b * (dsel * picked_b * (1.0 - picked_b))[:, :, None], axis=1)
    dnormed = jnp.dot(dlogit, table.astype(jnp.float32).T, precision=lax.Precision.HIGHEST)
    for k in range(top):
        dnormed = dnormed + gate_b[:, k : k + 1] * plan.home(masks_b[k], back_x)
    scaled = dnormed * gain
    inner = jnp.mean(scaled * wide_b, axis=-1, keepdims=True)
    dx_b = grads_b.astype(jnp.float32) + inv_b * scaled - wide_b * inv_b**3 * inner
    bwd_next = passed_along(dx_b.astype(jnp.bfloat16)[None], "pipe", -1)
    return (fwd_next, bwd_next)


def solution(mesh):
    placed = (
        P("pipe", "expert", None),
        P("pipe", "expert", None),
        P("pipe", "expert", None),
        P("pipe", None),
        P("pipe", None, None),
        P("pipe", None, "expert"),
        P("pipe", "expert", None),
        P("pipe", "expert", None),
        P("pipe", "expert", None),
    )
    return jax.shard_map(
        on_device,
        mesh=mesh,
        in_specs=placed,
        out_specs=(P("pipe", "expert", None), P("pipe", "expert", None)),
        check_vma=False,
    )
```

```python
import jax
import jax.numpy as jnp
from jax import lax
from jax.sharding import PartitionSpec as P

HALVES = 2
EPS = 1e-06
ROUTE_SCALE = 2.5


def partner(shard, axis, bit):
    return lax.ppermute(shard, axis, [(i, i ^ 1 << bit) for i in range(lax.axis_size(axis))])


def passed_along(block, axis, distance):
    devices = range(lax.axis_size(axis))
    route = [((i - distance) % len(devices), i) for i in devices]
    return lax.ppermute(block, axis, route)


def normalize(acts, gain):
    wide = acts.astype(jnp.float32)
    inverse = lax.rsqrt(jnp.mean(wide * wide, axis=-1, keepdims=True) + EPS)
    return (wide, inverse, (wide * inverse * gain).astype(jnp.bfloat16))


def gating(normed, table, choose):
    logits = jnp.dot(normed, table, preferred_element_type=jnp.float32)
    affinity = jax.nn.sigmoid(logits)
    onehot = (
        choose[:, :, None] == jnp.arange(table.shape[1], dtype=jnp.int32)[None, None, :]
    ).astype(jnp.float32)
    picked = jnp.sum(onehot * affinity[:, None, :], axis=2)
    total = jnp.sum(picked, axis=1, keepdims=True)
    return (onehot, picked, total, ROUTE_SCALE * picked / total)


ROWS = 16


class Layout:
    def __init__(self, width, half_cap, devices):
        self.width, self.half_cap, self.devices = width, half_cap, devices
        self.full, self.left = half_cap // ROWS, half_cap % ROWS
        self.pieces = ROWS // self.left if self.left else 1
        if self.left and (ROWS % self.left or width % (128 * self.pieces)):
            self.full, self.left, self.pieces = self.full + 1, 0, 1
        self.part = width // self.pieces
        self.columns = self.full * width + (self.part if self.left else 0)

    def masks(self, where):
        block = jnp.arange(self.devices * ROWS, dtype=jnp.int32)
        to, row = lax.axis_index("expert") ^ (block // ROWS), block % ROWS
        first = to * self.half_cap
        found = []
        for group in range(self.full):
            slot = group * ROWS + row
            place = jnp.where(slot < self.half_cap, first + slot, -1)
            found.append((place[:, None] == where[None, :]).astype(jnp.bfloat16))
        for piece in range(self.pieces if self.left else 0):
            slot = self.full * ROWS + row % self.left
            place = jnp.where(row // self.left == piece, first + slot, -1)
            found.append((place[:, None] == where[None, :]).astype(jnp.bfloat16))
        return found

    def parts(self, rows):
        return [rows[:, c * self.part : (c + 1) * self.part] for c in range(self.pieces)]

    def dispatch(self, masks, rows):
        cols = [pick(m, rows) for m in masks[: self.full]]
        if self.left:
            cols.append(
                pick(
                    jnp.concatenate(masks[self.full :], axis=1),
                    jnp.concatenate(self.parts(rows), axis=0),
                )
            )
        return jnp.concatenate(cols, axis=1)

    def lifts(self):
        slot = jnp.arange(self.devices * self.left, dtype=jnp.int32)
        block = jnp.arange(self.devices * ROWS, dtype=jnp.int32)
        at = (slot // self.left) * ROWS + slot % self.left
        return [
            (at[:, None] + c * self.left == block[None, :]).astype(jnp.bfloat16)
            for c in range(self.pieces)
        ]

    def unpack(self, packed):
        rows = [packed[:, g * self.width : (g + 1) * self.width] for g in range(self.full)]
        if self.left:
            tail = packed[:, self.full * self.width : self.columns]
            rows.append(jnp.concatenate([pick(m, tail) for m in self.lifts()], axis=1))
        return jnp.concatenate(rows, axis=0)

    def pack(self, rows):
        size = self.devices * ROWS
        cols = [rows[g * size : (g + 1) * size] for g in range(self.full)]
        if self.left:
            tail = rows[self.full * size :]
            cols.append(
                sum(back_to_tokens(m, p) for m, p in zip(self.lifts(), self.parts(tail))).astype(
                    jnp.bfloat16
                )
            )
        return jnp.concatenate(cols, axis=1)

    def numbers(self, values):
        size = self.devices * ROWS
        cols = [values[g * size : (g + 1) * size] for g in range(self.full)]
        if self.left:
            tail = values[self.full * size :]
            cols.append(jnp.sum(self.lifts()[0].astype(jnp.float32) * tail[:, None], axis=0))
        both = jnp.stack(cols, axis=1)
        high = lax.reduce_precision(both, 8, 7)
        split = jnp.concatenate([high, both - high], axis=1)
        return jnp.pad(split, ((0, 0), (0, -split.shape[1] % 128))).astype(jnp.bfloat16)

    def numbers_home(self, masks, split):
        count = self.full + (1 if self.left else 0)
        wide = split.astype(jnp.float32)
        return sum(
            jnp.sum(masks[g].astype(jnp.float32) * (wide[:, g] + wide[:, count + g])[:, None], axis=0)
            for g in range(count)
        )

    def home(self, masks, packed):
        out = sum(
            back_to_tokens(masks[g], packed[:, g * self.width : (g + 1) * self.width])
            for g in range(self.full)
        )
        if self.left:
            tail = packed[:, self.full * self.width : self.columns]
            out = out + jnp.concatenate(
                [back_to_tokens(m, tail) for m in masks[self.full :]], axis=1
            )
        return out

    def swap(self, packed):
        got = {0: packed[:ROWS]}
        for j in sorted(range(1, self.devices), key=lambda j: (-(j >> 1).bit_length(), -(j & 1), -j)):
            route = [(i, i ^ j) for i in range(self.devices)]
            got[j] = lax.ppermute(packed[j * ROWS : (j + 1) * ROWS], "expert", route)
        return [got[j] for j in range(self.devices)]


def joined(blocks, after=()):
    if len(after):
        blocks = lax.optimization_barrier((list(blocks), list(after)))[0]
    return jnp.concatenate(blocks, axis=0)


def slots_of(choose, experts, capacity):
    tok_rows, top = choose.shape
    flat = choose.reshape(-1)
    onehot = (flat[:, None] == jnp.arange(experts, dtype=jnp.int32)[None, :]).astype(jnp.bfloat16)
    at = jnp.arange(tok_rows * top, dtype=jnp.int32)
    earlier = (at[None, :] < at[:, None]).astype(jnp.bfloat16)
    before = jnp.dot(earlier, onehot, preferred_element_type=jnp.float32)
    slot = jnp.sum(before * onehot.astype(jnp.float32), axis=1).astype(jnp.int32)
    return (flat * capacity + slot).reshape(tok_rows, top)


def pick(mask, rows):
    return jnp.dot(mask, rows, preferred_element_type=jnp.float32).astype(jnp.bfloat16)


def back_to_tokens(mask, rows):
    return lax.dot_general(mask, rows, (((0,), (0,)), ((), ())), preferred_element_type=jnp.float32)


def on_device(
    fwd_acts, bwd_saved, bwd_grads, norm_gain, router, w_up, w_down, fwd_experts, bwd_experts
):
    gain = norm_gain[0]
    table = router[0]
    width = fwd_acts.shape[2]
    tok_rows = fwd_acts.shape[1]
    experts = table.shape[1]
    top = fwd_experts.shape[2]
    capacity = 9 * tok_rows * top // (8 * experts)
    half_cap = capacity // HALVES
    devices = lax.axis_size("expert")
    plan = Layout(width, half_cap, devices)
    ups = [w_up[0], partner(w_up[0], "expert", 0)]
    downs = [w_down[0], partner(w_down[0], "expert", 0)]

    choose_a = fwd_experts[0]
    where_a = slots_of(choose_a, experts, capacity)
    masks_a = [plan.masks(where_a[:, k]) for k in range(top)]
    wide_a, inv_a, normed_a = normalize(fwd_acts[0], gain)
    spread_a = [sum(each) for each in zip(*masks_a)]
    got_a = plan.unpack(joined(plan.swap(plan.dispatch(spread_a, normed_a))))
    _, _, _, gate_a = gating(normed_a, table, choose_a)

    choose_b = bwd_experts[0]
    grads_b = bwd_grads[0]
    where_b = slots_of(choose_b, experts, capacity)
    masks_b = [plan.masks(where_b[:, k]) for k in range(top)]
    wide_b, inv_b, normed_b = normalize(bwd_saved[0], gain)
    spread_b = [sum(each) for each in zip(*masks_b)]
    blocks_x = plan.swap(plan.dispatch(spread_b, normed_b))
    sent_g = plan.dispatch(spread_b, grads_b)
    onehot_b, picked_b, total_b, gate_b = gating(normed_b, table, choose_b)

    y = jnp.zeros((got_a.shape[0], width), jnp.float32)
    for up, down in zip(ups, downs):
        hidden = jax.nn.silu(jnp.dot(got_a, up, preferred_element_type=jnp.float32))
        y += jnp.dot(hidden.astype(jnp.bfloat16), down, preferred_element_type=jnp.float32)
    sent_a = plan.pack(y.astype(jnp.bfloat16))

    sent_g, sent_a = lax.optimization_barrier((sent_g, sent_a))
    blocks_g = plan.swap(sent_g)
    got_x = plan.unpack(joined(blocks_x, [sent_a]))
    pres = [jnp.dot(got_x, up, preferred_element_type=jnp.float32) for up in ups]
    pres, sent_a = lax.optimization_barrier((pres, sent_a))
    back_a = plan.swap(sent_a)
    got_g = plan.unpack(joined(blocks_g, pres))

    dx = jnp.zeros((got_a.shape[0], width), jnp.float32)
    dgate_rows = jnp.zeros((got_a.shape[0],), jnp.float32)
    for pre, up, down in zip(pres, ups, downs):
        sigma = jax.nn.sigmoid(pre)
        hidden = (pre * sigma).astype(jnp.bfloat16).astype(jnp.float32)
        back = lax.dot_general(
            got_g, down, (((1,), (1,)), ((), ())), preferred_element_type=jnp.float32
        )
        dgate_rows += jnp.sum(hidden * back, axis=1)
        dpre = (back * sigma * (1.0 + pre * (1.0 - sigma))).astype(jnp.bfloat16)
        dx += lax.dot_general(dpre, up, (((1,), (1,)), ((), ())), preferred_element_type=jnp.float32)
    sent_x = jnp.concatenate([plan.pack(dx.astype(jnp.bfloat16)), plan.numbers(dgate_rows)], axis=1)
    back_x = joined(plan.swap(sent_x))
    back_a = joined(back_a, [sent_x])

    out_a = wide_a
    for k in range(top):
        out_a = out_a + gate_a[:, k : k + 1] * plan.home(masks_a[k], back_a)
    fwd_next = passed_along(out_a.astype(jnp.bfloat16)[None], "pipe", 1)

    split = back_x[:, plan.columns :]
    dgate = jnp.stack([plan.numbers_home(m, split) for m in masks_b], axis=1)
    dsel = ROUTE_SCALE / total_b * (
        dgate - jnp.sum(dgate * picked_b, axis=1, keepdims=True) / total_b
    )
    dlogit = jnp.sum(onehot_b * (dsel * picked_b * (1.0 - picked_b))[:, :, None], axis=1)
    dnormed = jnp.dot(dlogit, table.astype(jnp.float32).T, precision=lax.Precision.HIGHEST)
    for k in range(top):
        dnormed = dnormed + gate_b[:, k : k + 1] * plan.home(masks_b[k], back_x)
    scaled = dnormed * gain
    inner = jnp.mean(scaled * wide_b, axis=-1, keepdims=True)
    dx_b = grads_b.astype(jnp.float32) + inv_b * scaled - wide_b * inv_b**3 * inner
    bwd_next = passed_along(dx_b.astype(jnp.bfloat16)[None], "pipe", -1)
    return (fwd_next, bwd_next)


def solution(mesh):
    placed = (
        P("pipe", "expert", None),
        P("pipe", "expert", None),
        P("pipe", "expert", None),
        P("pipe", None),
        P("pipe", None, None),
        P("pipe", None, "expert"),
        P("pipe", "expert", None),
        P("pipe", "expert", None),
        P("pipe", "expert", None),
    )
    return jax.shard_map(
        on_device,
        mesh=mesh,
        in_specs=placed,
        out_specs=(P("pipe", "expert", None), P("pipe", "expert", None)),
        check_vma=False,
    )
```

```python
import jax
import jax.numpy as jnp
from jax import lax
from jax.sharding import PartitionSpec as P

HALVES = 2
EPS = 1e-06
ROUTE_SCALE = 2.5


def partner(shard, axis, bit):
    return lax.ppermute(shard, axis, [(i, i ^ 1 << bit) for i in range(lax.axis_size(axis))])


def passed_along(block, axis, distance):
    devices = range(lax.axis_size(axis))
    route = [((i - distance) % len(devices), i) for i in devices]
    return lax.ppermute(block, axis, route)


def normalize(acts, gain):
    wide = acts.astype(jnp.float32)
    inverse = lax.rsqrt(jnp.mean(wide * wide, axis=-1, keepdims=True) + EPS)
    return (wide, inverse, (wide * inverse * gain).astype(jnp.bfloat16))


def gating(normed, table, choose):
    logits = jnp.dot(normed, table, preferred_element_type=jnp.float32)
    affinity = jax.nn.sigmoid(logits)
    onehot = (
        choose[:, :, None] == jnp.arange(table.shape[1], dtype=jnp.int32)[None, None, :]
    ).astype(jnp.float32)
    picked = jnp.sum(onehot * affinity[:, None, :], axis=2)
    total = jnp.sum(picked, axis=1, keepdims=True)
    return (onehot, picked, total, ROUTE_SCALE * picked / total)


ROWS = 16


class Layout:
    def __init__(self, width, capacity, pairs):
        self.width, self.capacity, self.pairs = width, capacity, pairs
        self.full, self.left = capacity // ROWS, capacity % ROWS
        self.pieces = ROWS // self.left if self.left else 1
        if self.left and (ROWS % self.left or width % (128 * self.pieces)):
            self.full, self.left, self.pieces = self.full + 1, 0, 1
        self.part = width // self.pieces
        self.columns = self.full * width + (self.part if self.left else 0)

    def masks(self, where):
        block = jnp.arange(self.pairs * ROWS, dtype=jnp.int32)
        to, row = lax.axis_index("expert") // HALVES ^ (block // ROWS), block % ROWS
        first = to * self.capacity
        found = []
        for group in range(self.full):
            slot = group * ROWS + row
            place = jnp.where(slot < self.capacity, first + slot, -1)
            found.append((place[:, None] == where[None, :]).astype(jnp.bfloat16))
        for piece in range(self.pieces if self.left else 0):
            slot = self.full * ROWS + row % self.left
            place = jnp.where(row // self.left == piece, first + slot, -1)
            found.append((place[:, None] == where[None, :]).astype(jnp.bfloat16))
        return found

    def parts(self, rows):
        return [rows[:, c * self.part : (c + 1) * self.part] for c in range(self.pieces)]

    def dispatch(self, masks, rows):
        cols = [pick(m, rows) for m in masks[: self.full]]
        if self.left:
            cols.append(
                pick(
                    jnp.concatenate(masks[self.full :], axis=1),
                    jnp.concatenate(self.parts(rows), axis=0),
                )
            )
        return jnp.concatenate(cols, axis=1)

    def lifts(self):
        slot = jnp.arange(self.pairs * self.left, dtype=jnp.int32)
        block = jnp.arange(self.pairs * ROWS, dtype=jnp.int32)
        at = (slot // self.left) * ROWS + slot % self.left
        return [
            (at[:, None] + c * self.left == block[None, :]).astype(jnp.bfloat16)
            for c in range(self.pieces)
        ]

    def unpack(self, packed):
        rows = [packed[:, g * self.width : (g + 1) * self.width] for g in range(self.full)]
        if self.left:
            tail = packed[:, self.full * self.width : self.columns]
            rows.append(jnp.concatenate([pick(m, tail) for m in self.lifts()], axis=1))
        return jnp.concatenate(rows, axis=0)

    def pack(self, rows):
        size = self.pairs * ROWS
        cols = [rows[g * size : (g + 1) * size] for g in range(self.full)]
        if self.left:
            tail = rows[self.full * size :]
            cols.append(
                sum(back_to_tokens(m, p) for m, p in zip(self.lifts(), self.parts(tail))).astype(
                    jnp.bfloat16
                )
            )
        return jnp.concatenate(cols, axis=1)

    def numbers(self, values):
        size = self.pairs * ROWS
        cols = [values[g * size : (g + 1) * size] for g in range(self.full)]
        if self.left:
            tail = values[self.full * size :]
            cols.append(jnp.sum(self.lifts()[0].astype(jnp.float32) * tail[:, None], axis=0))
        both = jnp.stack(cols, axis=1)
        high = lax.reduce_precision(both, 8, 7)
        split = jnp.concatenate([high, both - high], axis=1)
        return jnp.pad(split, ((0, 0), (0, -split.shape[1] % 128))).astype(jnp.bfloat16)

    def numbers_home(self, masks, split):
        count = self.full + (1 if self.left else 0)
        wide = split.astype(jnp.float32)
        return sum(
            jnp.sum(masks[g].astype(jnp.float32) * (wide[:, g] + wide[:, count + g])[:, None], axis=0)
            for g in range(count)
        )

    def home(self, masks, packed):
        out = sum(
            back_to_tokens(masks[g], packed[:, g * self.width : (g + 1) * self.width])
            for g in range(self.full)
        )
        if self.left:
            tail = packed[:, self.full * self.width : self.columns]
            out = out + jnp.concatenate(
                [back_to_tokens(m, tail) for m in masks[self.full :]], axis=1
            )
        return out

    def swap(self, packed):
        got = {0: packed[:ROWS]}
        for j in range(self.pairs - 1, 0, -1):
            route = [(i, i ^ j * HALVES) for i in range(self.pairs * HALVES)]
            got[j] = lax.ppermute(packed[j * ROWS : (j + 1) * ROWS], "expert", route)
        return [got[j] for j in range(self.pairs)]


def joined(blocks, after=()):
    if len(after):
        blocks = lax.optimization_barrier((list(blocks), list(after)))[0]
    return jnp.concatenate(blocks, axis=0)


def slots_of(choose, experts, capacity):
    tok_rows, top = choose.shape
    flat = choose.reshape(-1)
    onehot = (flat[:, None] == jnp.arange(experts, dtype=jnp.int32)[None, :]).astype(jnp.bfloat16)
    at = jnp.arange(tok_rows * top, dtype=jnp.int32)
    earlier = (at[None, :] < at[:, None]).astype(jnp.bfloat16)
    before = jnp.dot(earlier, onehot, preferred_element_type=jnp.float32)
    slot = jnp.sum(before * onehot.astype(jnp.float32), axis=1).astype(jnp.int32)
    return (flat * capacity + slot).reshape(tok_rows, top)


def pick(mask, rows):
    return jnp.dot(mask, rows, preferred_element_type=jnp.float32).astype(jnp.bfloat16)


def back_to_tokens(mask, rows):
    return lax.dot_general(mask, rows, (((0,), (0,)), ((), ())), preferred_element_type=jnp.float32)


def on_device(
    fwd_acts, bwd_saved, bwd_grads, norm_gain, router, w_up, w_down, fwd_experts, bwd_experts
):
    gain = norm_gain[0]
    table = router[0]
    width = fwd_acts.shape[2]
    tok_rows = fwd_acts.shape[1]
    experts = table.shape[1]
    top = fwd_experts.shape[2]
    capacity = 9 * tok_rows * top // (8 * experts)
    plan = Layout(width, capacity, lax.axis_size("expert") // HALVES)
    ups = [w_up[0], partner(w_up[0], "expert", 0)]
    downs = [w_down[0], partner(w_down[0], "expert", 0)]

    choose_a = fwd_experts[0]
    where_a = slots_of(choose_a, experts, capacity)
    masks_a = [plan.masks(where_a[:, k]) for k in range(top)]
    wide_a, inv_a, normed_a = normalize(fwd_acts[0], gain)
    spread_a = [sum(each) for each in zip(*masks_a)]
    got_a = plan.unpack(joined(plan.swap(plan.dispatch(spread_a, normed_a))))
    _, _, _, gate_a = gating(normed_a, table, choose_a)

    choose_b = bwd_experts[0]
    grads_b = bwd_grads[0]
    where_b = slots_of(choose_b, experts, capacity)
    masks_b = [plan.masks(where_b[:, k]) for k in range(top)]
    wide_b, inv_b, normed_b = normalize(bwd_saved[0], gain)
    spread_b = [sum(each) for each in zip(*masks_b)]
    blocks_x = plan.swap(plan.dispatch(spread_b, normed_b))
    sent_g = plan.dispatch(spread_b, grads_b)
    onehot_b, picked_b, total_b, gate_b = gating(normed_b, table, choose_b)

    y = jnp.zeros((got_a.shape[0], width), jnp.float32)
    for up, down in zip(ups, downs):
        hidden = jax.nn.silu(jnp.dot(got_a, up, preferred_element_type=jnp.float32))
        y += jnp.dot(hidden.astype(jnp.bfloat16), down, preferred_element_type=jnp.float32)
    sent_a = plan.pack(y.astype(jnp.bfloat16))

    sent_g, sent_a = lax.optimization_barrier((sent_g, sent_a))
    blocks_g = plan.swap(sent_g)
    got_x = plan.unpack(joined(blocks_x, [sent_a]))
    pres = [jnp.dot(got_x, up, preferred_element_type=jnp.float32) for up in ups]
    pres, sent_a = lax.optimization_barrier((pres, sent_a))
    back_a = plan.swap(sent_a)
    got_g = plan.unpack(joined(blocks_g, pres))

    dx = jnp.zeros((got_a.shape[0], width), jnp.float32)
    dgate_rows = jnp.zeros((got_a.shape[0],), jnp.float32)
    for pre, up, down in zip(pres, ups, downs):
        sigma = jax.nn.sigmoid(pre)
        hidden = (pre * sigma).astype(jnp.bfloat16).astype(jnp.float32)
        back = lax.dot_general(
            got_g, down, (((1,), (1,)), ((), ())), preferred_element_type=jnp.float32
        )
        dgate_rows += jnp.sum(hidden * back, axis=1)
        dpre = (back * sigma * (1.0 + pre * (1.0 - sigma))).astype(jnp.bfloat16)
        dx += lax.dot_general(dpre, up, (((1,), (1,)), ((), ())), preferred_element_type=jnp.float32)
    sent_x = jnp.concatenate([plan.pack(dx.astype(jnp.bfloat16)), plan.numbers(dgate_rows)], axis=1)
    back_x = joined(plan.swap(sent_x))
    back_a = joined(back_a, [sent_x])

    out_a = wide_a
    for k in range(top):
        out_a = out_a + gate_a[:, k : k + 1] * plan.home(masks_a[k], back_a)
    fwd_next = passed_along(out_a.astype(jnp.bfloat16)[None], "pipe", 1)

    split = back_x[:, plan.columns :]
    dgate = jnp.stack([plan.numbers_home(m, split) for m in masks_b], axis=1)
    dsel = ROUTE_SCALE / total_b * (
        dgate - jnp.sum(dgate * picked_b, axis=1, keepdims=True) / total_b
    )
    dlogit = jnp.sum(onehot_b * (dsel * picked_b * (1.0 - picked_b))[:, :, None], axis=1)
    dnormed = jnp.dot(dlogit, table.astype(jnp.float32).T, precision=lax.Precision.HIGHEST)
    for k in range(top):
        dnormed = dnormed + gate_b[:, k : k + 1] * plan.home(masks_b[k], back_x)
    scaled = dnormed * gain
    inner = jnp.mean(scaled * wide_b, axis=-1, keepdims=True)
    dx_b = grads_b.astype(jnp.float32) + inv_b * scaled - wide_b * inv_b**3 * inner
    bwd_next = passed_along(dx_b.astype(jnp.bfloat16)[None], "pipe", -1)
    return (fwd_next, bwd_next)


def solution(mesh):
    placed = (
        P("pipe", "expert", None),
        P("pipe", "expert", None),
        P("pipe", "expert", None),
        P("pipe", None),
        P("pipe", None, None),
        P("pipe", None, "expert"),
        P("pipe", "expert", None),
        P("pipe", "expert", None),
        P("pipe", "expert", None),
    )
    return jax.shard_map(
        on_device,
        mesh=mesh,
        in_specs=placed,
        out_specs=(P("pipe", "expert", None), P("pipe", "expert", None)),
        check_vma=False,
    )
```

```python
import jax
import jax.numpy as jnp
from jax import lax
from jax.sharding import PartitionSpec as P

HALVES = 2
EPS = 1e-06
ROUTE_SCALE = 2.5


def partner(shard, axis, bit):
    return lax.ppermute(shard, axis, [(i, i ^ 1 << bit) for i in range(lax.axis_size(axis))])


def passed_along(block, axis, distance):
    devices = range(lax.axis_size(axis))
    route = [((i - distance) % len(devices), i) for i in devices]
    return lax.ppermute(block, axis, route)


def normalize(acts, gain):
    wide = acts.astype(jnp.float32)
    inverse = lax.rsqrt(jnp.mean(wide * wide, axis=-1, keepdims=True) + EPS)
    return (wide, inverse, (wide * inverse * gain).astype(jnp.bfloat16))


def gating(normed, table, choose):
    logits = jnp.dot(normed, table, preferred_element_type=jnp.float32)
    affinity = jax.nn.sigmoid(logits)
    onehot = (
        choose[:, :, None] == jnp.arange(table.shape[1], dtype=jnp.int32)[None, None, :]
    ).astype(jnp.float32)
    picked = jnp.sum(onehot * affinity[:, None, :], axis=2)
    total = jnp.sum(picked, axis=1, keepdims=True)
    return (onehot, picked, total, ROUTE_SCALE * picked / total)


ROWS = 16


class Layout:
    def __init__(self, width, capacity, pairs):
        self.width, self.capacity, self.pairs = width, capacity, pairs
        self.full, self.left = capacity // ROWS, capacity % ROWS
        self.pieces = ROWS // self.left if self.left else 1
        if self.left and (ROWS % self.left or width % (128 * self.pieces)):
            self.full, self.left, self.pieces = self.full + 1, 0, 1
        self.part = width // self.pieces
        self.columns = self.full * width + (self.part if self.left else 0)

    def masks(self, where):
        block = jnp.arange(self.pairs * ROWS, dtype=jnp.int32)
        to, row = lax.axis_index("expert") // HALVES ^ (block // ROWS), block % ROWS
        first = to * self.capacity
        found = []
        for group in range(self.full):
            slot = group * ROWS + row
            place = jnp.where(slot < self.capacity, first + slot, -1)
            found.append((place[:, None] == where[None, :]).astype(jnp.bfloat16))
        for piece in range(self.pieces if self.left else 0):
            slot = self.full * ROWS + row % self.left
            place = jnp.where(row // self.left == piece, first + slot, -1)
            found.append((place[:, None] == where[None, :]).astype(jnp.bfloat16))
        return found

    def parts(self, rows):
        return [rows[:, c * self.part : (c + 1) * self.part] for c in range(self.pieces)]

    def dispatch(self, masks, rows):
        cols = [pick(m, rows) for m in masks[: self.full]]
        if self.left:
            cols.append(
                pick(
                    jnp.concatenate(masks[self.full :], axis=1),
                    jnp.concatenate(self.parts(rows), axis=0),
                )
            )
        return jnp.concatenate(cols, axis=1)

    def lifts(self):
        slot = jnp.arange(self.pairs * self.left, dtype=jnp.int32)
        block = jnp.arange(self.pairs * ROWS, dtype=jnp.int32)
        at = (slot // self.left) * ROWS + slot % self.left
        return [
            (at[:, None] + c * self.left == block[None, :]).astype(jnp.bfloat16)
            for c in range(self.pieces)
        ]

    def unpack(self, packed):
        rows = [packed[:, g * self.width : (g + 1) * self.width] for g in range(self.full)]
        if self.left:
            tail = packed[:, self.full * self.width : self.columns]
            rows.append(jnp.concatenate([pick(m, tail) for m in self.lifts()], axis=1))
        return jnp.concatenate(rows, axis=0)

    def pack(self, rows):
        size = self.pairs * ROWS
        cols = [rows[g * size : (g + 1) * size] for g in range(self.full)]
        if self.left:
            tail = rows[self.full * size :]
            cols.append(
                sum(back_to_tokens(m, p) for m, p in zip(self.lifts(), self.parts(tail))).astype(
                    jnp.bfloat16
                )
            )
        return jnp.concatenate(cols, axis=1)

    def numbers(self, values):
        size = self.pairs * ROWS
        cols = [values[g * size : (g + 1) * size] for g in range(self.full)]
        if self.left:
            tail = values[self.full * size :]
            cols.append(jnp.sum(self.lifts()[0].astype(jnp.float32) * tail[:, None], axis=0))
        both = jnp.stack(cols, axis=1)
        high = lax.reduce_precision(both, 8, 7)
        split = jnp.concatenate([high, both - high], axis=1)
        return jnp.pad(split, ((0, 0), (0, -split.shape[1] % 128))).astype(jnp.bfloat16)

    def numbers_home(self, masks, split):
        count = self.full + (1 if self.left else 0)
        wide = split.astype(jnp.float32)
        return sum(
            jnp.sum(masks[g].astype(jnp.float32) * (wide[:, g] + wide[:, count + g])[:, None], axis=0)
            for g in range(count)
        )

    def home(self, masks, packed):
        out = sum(
            back_to_tokens(masks[g], packed[:, g * self.width : (g + 1) * self.width])
            for g in range(self.full)
        )
        if self.left:
            tail = packed[:, self.full * self.width : self.columns]
            out = out + jnp.concatenate(
                [back_to_tokens(m, tail) for m in masks[self.full :]], axis=1
            )
        return out

    def swap(self, packed):
        got = {0: packed[:ROWS]}
        for j in range(self.pairs - 1, 0, -1):
            route = [(i, i ^ j * HALVES) for i in range(self.pairs * HALVES)]
            got[j] = lax.ppermute(packed[j * ROWS : (j + 1) * ROWS], "expert", route)
        return [got[j] for j in range(self.pairs)]


def joined(blocks, after=()):
    if len(after):
        blocks = lax.optimization_barrier((list(blocks), list(after)))[0]
    return jnp.concatenate(blocks, axis=0)


def slots_of(choose, experts, capacity):
    tok_rows, top = choose.shape
    flat = choose.reshape(-1)
    onehot = (flat[:, None] == jnp.arange(experts, dtype=jnp.int32)[None, :]).astype(jnp.bfloat16)
    at = jnp.arange(tok_rows * top, dtype=jnp.int32)
    earlier = (at[None, :] < at[:, None]).astype(jnp.bfloat16)
    before = jnp.dot(earlier, onehot, preferred_element_type=jnp.float32)
    slot = jnp.sum(before * onehot.astype(jnp.float32), axis=1).astype(jnp.int32)
    return (flat * capacity + slot).reshape(tok_rows, top)


def pick(mask, rows):
    return jnp.dot(mask, rows, preferred_element_type=jnp.float32).astype(jnp.bfloat16)


def back_to_tokens(mask, rows):
    return lax.dot_general(mask, rows, (((0,), (0,)), ((), ())), preferred_element_type=jnp.float32)


def on_device(
    fwd_acts, bwd_saved, bwd_grads, norm_gain, router, w_up, w_down, fwd_experts, bwd_experts
):
    gain = norm_gain[0]
    table = router[0]
    width = fwd_acts.shape[2]
    tok_rows = fwd_acts.shape[1]
    experts = table.shape[1]
    top = fwd_experts.shape[2]
    capacity = 9 * tok_rows * top // (8 * experts)
    plan = Layout(width, capacity, lax.axis_size("expert") // HALVES)
    ups = [w_up[0], partner(w_up[0], "expert", 0)]
    downs = [w_down[0], partner(w_down[0], "expert", 0)]

    choose_a = fwd_experts[0]
    where_a = slots_of(choose_a, experts, capacity)
    masks_a = [plan.masks(where_a[:, k]) for k in range(top)]
    wide_a, inv_a, normed_a = normalize(fwd_acts[0], gain)
    spread_a = [sum(each) for each in zip(*masks_a)]
    got_a = plan.unpack(joined(plan.swap(plan.dispatch(spread_a, normed_a))))
    _, _, _, gate_a = gating(normed_a, table, choose_a)

    choose_b = bwd_experts[0]
    grads_b = bwd_grads[0]
    where_b = slots_of(choose_b, experts, capacity)
    masks_b = [plan.masks(where_b[:, k]) for k in range(top)]
    wide_b, inv_b, normed_b = normalize(bwd_saved[0], gain)
    spread_b = [sum(each) for each in zip(*masks_b)]
    blocks_x = plan.swap(plan.dispatch(spread_b, normed_b))
    sent_g = plan.dispatch(spread_b, grads_b)
    onehot_b, picked_b, total_b, gate_b = gating(normed_b, table, choose_b)

    y = jnp.zeros((got_a.shape[0], width), jnp.float32)
    for up, down in zip(ups, downs):
        hidden = jax.nn.silu(jnp.dot(got_a, up, preferred_element_type=jnp.float32))
        y += jnp.dot(hidden.astype(jnp.bfloat16), down, preferred_element_type=jnp.float32)
    sent_a = plan.pack(y.astype(jnp.bfloat16))

    blocks_g = plan.swap(sent_g)
    got_x = plan.unpack(joined(blocks_x, [sent_a]))
    pres = [jnp.dot(got_x, up, preferred_element_type=jnp.float32) for up in ups]
    pres, sent_a = lax.optimization_barrier((pres, sent_a))
    back_a = plan.swap(sent_a)
    got_g = plan.unpack(joined(blocks_g, pres))

    dx = jnp.zeros((got_a.shape[0], width), jnp.float32)
    dgate_rows = jnp.zeros((got_a.shape[0],), jnp.float32)
    for pre, up, down in zip(pres, ups, downs):
        sigma = jax.nn.sigmoid(pre)
        hidden = (pre * sigma).astype(jnp.bfloat16).astype(jnp.float32)
        back = lax.dot_general(
            got_g, down, (((1,), (1,)), ((), ())), preferred_element_type=jnp.float32
        )
        dgate_rows += jnp.sum(hidden * back, axis=1)
        dpre = (back * sigma * (1.0 + pre * (1.0 - sigma))).astype(jnp.bfloat16)
        dx += lax.dot_general(dpre, up, (((1,), (1,)), ((), ())), preferred_element_type=jnp.float32)
    sent_x = jnp.concatenate([plan.pack(dx.astype(jnp.bfloat16)), plan.numbers(dgate_rows)], axis=1)
    back_x = joined(plan.swap(sent_x))
    back_a = joined(back_a, [sent_x])

    out_a = wide_a
    for k in range(top):
        out_a = out_a + gate_a[:, k : k + 1] * plan.home(masks_a[k], back_a)
    fwd_next = passed_along(out_a.astype(jnp.bfloat16)[None], "pipe", 1)

    split = back_x[:, plan.columns :]
    dgate = jnp.stack([plan.numbers_home(m, split) for m in masks_b], axis=1)
    dsel = ROUTE_SCALE / total_b * (
        dgate - jnp.sum(dgate * picked_b, axis=1, keepdims=True) / total_b
    )
    dlogit = jnp.sum(onehot_b * (dsel * picked_b * (1.0 - picked_b))[:, :, None], axis=1)
    dnormed = jnp.dot(dlogit, table.astype(jnp.float32).T, precision=lax.Precision.HIGHEST)
    for k in range(top):
        dnormed = dnormed + gate_b[:, k : k + 1] * plan.home(masks_b[k], back_x)
    scaled = dnormed * gain
    inner = jnp.mean(scaled * wide_b, axis=-1, keepdims=True)
    dx_b = grads_b.astype(jnp.float32) + inv_b * scaled - wide_b * inv_b**3 * inner
    bwd_next = passed_along(dx_b.astype(jnp.bfloat16)[None], "pipe", -1)
    return (fwd_next, bwd_next)


def solution(mesh):
    placed = (
        P("pipe", "expert", None),
        P("pipe", "expert", None),
        P("pipe", "expert", None),
        P("pipe", None),
        P("pipe", None, None),
        P("pipe", None, "expert"),
        P("pipe", "expert", None),
        P("pipe", "expert", None),
        P("pipe", "expert", None),
    )
    return jax.shard_map(
        on_device,
        mesh=mesh,
        in_specs=placed,
        out_specs=(P("pipe", "expert", None), P("pipe", "expert", None)),
        check_vma=False,
    )
```
